32 devices in a mesh: gx: 8 (over z, x), gy: 4 (over y, core).
Axes of the slice: x: 2, y: 2, z: 4, core: 2. Of those that a mesh axis runs over, the one named last changes fastest.
Arguments:
- labels: int32 [48, 32, 256], P('gx', 'gy'), may hold values from 0 to 7
- permittivity_real: float32 [8], replicated, may hold values from 1 to 2.5
- permittivity_imag: float32 [8], replicated, may hold values from 0 to 0.5
- angles: float32 [360], replicated, may hold values from -3.140625 to 3.140625
- angle_pick: int32 [4], replicated, may hold values from 0 to 359
Outputs:
- scattered_field: float32 [2, 4, 48, 32, 256], P(None, None, 'gx', 'gy')
The draws below stay inside these ranges and needn't reach their ends.
All inputs are finite; a program needn't handle non-finite values.
Results may differ from the reference program's by a relative error of at most 0.000054.
Values sent between devices are 32-bit elements; how exact they have to be, the bound alone decides.
A program may use at most 64 MiB of HBM per device.

```python
import jax
import jax.numpy as jnp
from jax import lax

NZ = 256
COLS = 4
NANG = 360
MAT = 8
FINE_SWEEPS = 2
COARSE_SWEEPS = 4
NX = 48
NY = 32


def set_ends(result, stream_key, least, top_value):
    shape = result.shape
    spot = [jax.random.randint(jax.random.fold_in(stream_key, axis), (), 0, shape[axis]) for axis in range(len(shape))]
    result = result.at[tuple(spot)].set(least)
    longest = shape.index(max(shape))
    spot[longest] = (spot[longest] + 1) % shape[longest]
    return result.at[tuple(spot)].set(top_value)


def setup_inputs(seed: int = 0) -> dict:
    keys = jax.random.split(jax.random.key(seed), 6)
    return {
        "labels": set_ends(jax.random.randint(keys[0], (NX, NY, NZ), 0, MAT), jax.random.fold_in(keys[0], 1), 0, MAT - 1).astype(jnp.int32),
        "permittivity_real": jnp.clip(jax.random.uniform(keys[1], (MAT,), jnp.float32, 1.0, 2.5), 1.0, 2.5),
        "permittivity_imag": jnp.clip(jax.random.uniform(keys[2], (MAT,), jnp.float32, 0.0, 0.5), 0.0, 0.5),
        "angles": jnp.clip(jax.random.uniform(keys[3], (NANG,), jnp.float32, -3.140625, 3.140625), -3.140625, 3.140625),
        "angle_pick": set_ends(jax.random.randint(keys[4], (COLS,), 0, NANG), jax.random.fold_in(keys[4], 1), 0, NANG - 1).astype(jnp.int32),
    }


WEIGHTS = (128.0, -14.0, -3.0, -1.0)
DAMPING = 0.8
WAVE_SQUARED = 0.1
SHIFT_IMAG = 0.5
SOURCE_GAIN = 4.0

def stencil(padded):
    extent_x = padded.shape[-3] - 2
    extent_y = padded.shape[-2] - 2
    extent_z = padded.shape[-1] - 2
    summed = jnp.zeros(padded.shape[:-3] + (extent_x, extent_y, extent_z), padded.dtype)
    for offset_x in (0, 1, 2):
        for offset_y in (0, 1, 2):
            for offset_z in (0, 1, 2):
                weight = WEIGHTS[abs(offset_x - 1) + abs(offset_y - 1) + abs(offset_z - 1)]
                summed = summed + weight * padded[..., offset_x:offset_x + extent_x, offset_y:offset_y + extent_y, offset_z:offset_z + extent_z]
    return summed / 30.0

def complex_product(coefs, values):
    real_out = coefs[0] * values[0] - coefs[1] * values[1]
    imag_out = coefs[0] * values[1] + coefs[1] * values[0]
    return jnp.stack([real_out, imag_out])

def apply_operator(iterate, padded, medium, factor):
    laplace = stencil(padded) * factor
    return laplace - complex_product(medium, iterate)

def inverse_diagonal(medium, centre_weight):
    diag_real = centre_weight - medium[0]
    diag_imag = -medium[1]
    modulus = diag_real * diag_real + diag_imag * diag_imag
    return jnp.stack([diag_real / modulus, -diag_imag / modulus])

def pad_all(values):
    return jnp.pad(values, ((0, 0), (0, 0), (1, 1), (1, 1), (1, 1)))

def restrict_axis(values, along):
    planes = (values.shape[along] - 1) // 2
    low_side = lax.slice_in_dim(values, 0, 2 * planes, 2, along)
    centre = lax.slice_in_dim(values, 1, 2 * planes, 2, along)
    high_side = lax.slice_in_dim(values, 2, 2 * planes + 1, 2, along)
    return (low_side + 2.0 * centre + high_side) * 0.25

def prolong_axis(values, along):
    planes = values.shape[along] - 1
    lower_part = lax.slice_in_dim(values, 0, planes, 1, along)
    upper_part = lax.slice_in_dim(values, 1, planes + 1, 1, along)
    even_rows = (lower_part + upper_part) * 0.5
    stacked = jnp.stack([even_rows, upper_part], axis=along + 1)
    new_shape = list(values.shape)
    new_shape[along] = 2 * planes
    return stacked.reshape(new_shape)

def reference(labels, permittivity_real, permittivity_imag, angles, angle_pick):
    eps_real = permittivity_real[labels]
    eps_imag = permittivity_imag[labels]
    medium = WAVE_SQUARED * jnp.stack([eps_real + SHIFT_IMAG * eps_imag, eps_imag - SHIFT_IMAG * eps_real])
    incidence = angles[angle_pick]
    wavenumber = jnp.sqrt(WAVE_SQUARED)
    pos_x = jnp.arange(NX).astype(jnp.float32)
    pos_y = jnp.arange(NY).astype(jnp.float32)
    phases = wavenumber * (jnp.cos(incidence)[:, None, None] * pos_x[None, :, None] + jnp.sin(incidence)[:, None, None] * pos_y[None, None, :])
    phases = phases[..., None]
    contrast = eps_real - 1.0
    source = SOURCE_GAIN * jnp.stack([contrast * jnp.cos(phases) - eps_imag * jnp.sin(phases), contrast * jnp.sin(phases) + eps_imag * jnp.cos(phases)])
    inverse = inverse_diagonal(medium, 128.0 / 30.0)
    iterate = DAMPING * complex_product(inverse, source)
    for sweep_index in range(FINE_SWEEPS - 1):
        residual = source - apply_operator(iterate, pad_all(iterate), medium, 1.0)
        iterate = iterate + DAMPING * complex_product(inverse, residual)
    residual = source - apply_operator(iterate, pad_all(iterate), medium, 1.0)
    extended = jnp.pad(residual, ((0, 0), (0, 0), (0, 1), (0, 1), (0, 1)))
    coarse_rhs = restrict_axis(restrict_axis(restrict_axis(extended, 2), 3), 4)
    coarse_medium = medium[:, 1::2, 1::2, 1::2]
    coarse_inverse = inverse_diagonal(coarse_medium, 128.0 / 120.0)
    correction = DAMPING * complex_product(coarse_inverse, coarse_rhs)
    for sweep_index in range(COARSE_SWEEPS - 1):
        coarse_res = coarse_rhs - apply_operator(correction, pad_all(correction), coarse_medium, 0.25)
        correction = correction + DAMPING * complex_product(coarse_inverse, coarse_res)
    extended = jnp.pad(correction, ((0, 0), (0, 0), (1, 0), (1, 0), (1, 0)))
    fine_correction = prolong_axis(prolong_axis(prolong_axis(extended, 2), 3), 4)
    return iterate + fine_correction
```

```python
import functools

import jax
import jax.numpy as jnp
from jax import lax
from jax.experimental import pallas as pl
from jax.experimental.pallas import tpu as pltpu
from jax.sharding import PartitionSpec as P

MAT = 8
DAMPING = 0.8
WAVE_SQUARED = 0.1
SHIFT_IMAG = 0.5
SOURCE_GAIN = 4.0
CENTRE = 128.0 / 30.0
COARSE_CENTRE = 128.0 / 120.0
LOW, HIGH = 2, 3
DIRS = [(dx, dy) for dx in (-1, 0, 1) for dy in (-1, 0, 1) if (dx, dy) != (0, 0)]
f32 = jnp.float32


def windows(step, size, low, high):
    if step == 0:
        return low, low, size
    if step > 0:
        return size, 0, low
    return low, low + size, high


def shift_up(values, first):
    return jnp.where(first, 0.0, pltpu.roll(values, 1, 1))


def shift_down(values, last):
    return jnp.where(last, 0.0, pltpu.roll(values, values.shape[1] - 1, 1))


def plane_sums(centre, ends, y):
    side = ends[y] + (centre[y - 1] + centre[y + 1])
    diag = ends[y - 1] + ends[y + 1]
    return 14.0 * side + 3.0 * diag, 14.0 * centre[y] + (3.0 * side + diag)


def fine_neighbours(buf, x, rows, first, last):
    span = range(rows[0] - 1, rows[-1] + 2)
    halves = []
    for half in (0, 1):
        centre = {y: buf[x, y, half] for y in span}
        ends = {y: buf[x - 1, y, half] + buf[x + 1, y, half] for y in span}
        halves.append([plane_sums(centre, ends, y) for y in rows])
    for i, y in enumerate(rows):
        (in_even, out_even), (in_odd, out_odd) = halves[0][i], halves[1][i]
        yield (
            y,
            in_even + (out_odd + shift_up(out_odd, first)),
            in_odd + (out_even + shift_down(out_even, last)),
        )


def coarse_neighbours(buf, x, rows, first, last):
    span = range(rows[0] - 1, rows[-1] + 2)
    centre = {y: buf[x, y] for y in span}
    ends = {y: buf[x - 1, y] + buf[x + 1, y] for y in span}
    for y in rows:
        inner, outer = plane_sums(centre, ends, y)
        yield y, inner + (shift_up(outer, first) + shift_down(outer, last))


def cycle_kernel(
    nx, ny,
    labels_ref, eps_r_ref, eps_i_ref, angles_ref, pick_ref,
    iterate_ref, corr_ref,
    lab, tab, ctab, ewave, wave, it0, w, yz, c0, c1, c2,
    send_sems, recv_sems,
):
    sizex, sizey, sizez = labels_ref.shape
    nzc = sizez // 2
    cx, cy = sizex // 2, sizey // 2
    extx, exty = sizex + LOW + HIGH, sizey + LOW + HIGH
    px, py = lax.axis_index("gx"), lax.axis_index("gy")

    def there(dx, dy):
        ok = None
        for step, pos, count in ((dx, px, nx), (dy, py, ny)):
            if step:
                one = (pos > 0) if step < 0 else (pos < count - 1)
                ok = one if ok is None else jnp.logical_and(ok, one)
        return ok

    lab[...] = jnp.full(lab.shape, float(MAT), f32)
    c0[...] = jnp.zeros(c0.shape, f32)
    c2[...] = jnp.zeros(c2.shape, f32)
    barrier = pltpu.get_barrier_semaphore()
    for dx, dy in DIRS:
        @pl.when(there(dx, dy))
        def _():
            pl.semaphore_signal(
                barrier, inc=1, device_id=(px + dx, py + dy), device_id_type=pl.DeviceIdType.MESH
            )

    row = lax.broadcasted_iota(jnp.int32, (sizez, sizez), 0)
    col = lax.broadcasted_iota(jnp.int32, (sizez, sizez), 1)
    split = jnp.where(row == jnp.where(col < nzc, 2 * col, 2 * (col - nzc) + 1), 1.0, 0.0).astype(jnp.bfloat16)
    mine = labels_ref[...].astype(f32).reshape(sizex * sizey, sizez).astype(jnp.bfloat16)
    mine = jnp.dot(mine, split, preferred_element_type=f32)
    for x in range(sizex):
        for half in (0, 1):
            lab[x + LOW, pl.ds(2 * LOW + half, sizey, stride=2), :] = mine[
                x * sizey : (x + 1) * sizey, half * nzc : (half + 1) * nzc
            ]

    def exchange(phase, buf, sizes, low, high, fold):
        copies = []
        for d, (dx, dy) in enumerate(DIRS):
            fx, tx, lx = windows(dx, sizes[0], low, high)
            fy, ty, ly = windows(dy, sizes[1], low, high)
            out = pltpu.make_async_remote_copy(
                src_ref=buf.at[pl.ds(fx, lx), pl.ds(fold * fy, fold * ly)],
                dst_ref=buf.at[pl.ds(tx, lx), pl.ds(fold * ty, fold * ly)],
                send_sem=send_sems.at[phase, d],
                recv_sem=recv_sems.at[phase, d],
                device_id=(px + dx, py + dy),
                device_id_type=pl.DeviceIdType.MESH,
            )
            copies.append(out)
            pl.when(there(dx, dy))(out.start)
        return copies

    def finish(copies):
        for (dx, dy), copy in zip(DIRS, copies):
            pl.when(there(-dx, -dy))(copy.wait_recv)

    def finish_sends(copies):
        for (dx, dy), copy in zip(DIRS, copies):
            pl.when(there(dx, dy))(copy.wait_send)

    one = jnp.int32(1)
    besides_x = jnp.where(px > 0, one, 0) + jnp.where(px < nx - 1, one, 0)
    besides_y = jnp.where(py > 0, one, 0) + jnp.where(py < ny - 1, one, 0)
    pl.semaphore_wait(barrier, (besides_x + 1) * (besides_y + 1) - 1)
    sent_labels = exchange(0, lab, (sizex, sizey), LOW, HIGH, 2)

    lane = lax.broadcasted_iota(jnp.int32, (8, nzc), 1)
    field = lax.broadcasted_iota(jnp.int32, (8, nzc), 0)
    first, last = lane == 0, lane == nzc - 1
    imag = field >= 4
    sign = jnp.where(imag, 1.0, -1.0)
    column = field % 4
    incidence = jnp.zeros((8, nzc), f32)
    for c in range(4):
        incidence = jnp.where(column == c, angles_ref[pick_ref[c]], incidence)
    wavenumber = jnp.sqrt(jnp.full((8, nzc), WAVE_SQUARED, f32))
    on_x = lane < nzc // 2
    place = jnp.where(on_x, px * sizex - LOW + lane, py * sizey - LOW + lane - nzc // 2).astype(f32)
    arg = wavenumber * jnp.where(on_x, jnp.cos(incidence), jnp.sin(incidence)) * place
    cos_all, sin_all = jnp.cos(arg), jnp.sin(arg)
    one_all = jnp.where(imag, sin_all, cos_all)
    two_all = jnp.where(imag, cos_all, -sin_all)
    spread = lambda values, at: jnp.broadcast_to(values[:, at : at + 1], (8, nzc))
    for x in range(extx):
        ewave[x, 0] = spread(one_all, x)
        ewave[x, 1] = spread(two_all, x)
    along_y = [
        (spread(cos_all, nzc // 2 + y), spread(sin_all, nzc // 2 + y)) for y in range(exty)
    ]
    for y in range(exty):
        ewave[extx + y, 0], ewave[extx + y, 1] = along_y[y]

    def fill_wave(x, carry):
        wave_one, wave_two = ewave[x, 0], ewave[x, 1]
        for y in range(exty):
            cos_y, sin_y = ewave[extx + y, 0], ewave[extx + y, 1]
            wave[x, y, 0] = cos_y * wave_one + sin_y * wave_two
            wave[x, y, 1] = cos_y * wave_two - sin_y * wave_one
        return carry

    lax.fori_loop(0, extx, fill_wave, 0)
    eps_table = [(eps_r_ref[m], eps_i_ref[m]) for m in range(MAT)]
    finish(sent_labels)

    def media(label):
        eps_r = jnp.zeros(label.shape, f32)
        eps_i = jnp.zeros(label.shape, f32)
        for m in range(MAT):
            chosen = label == float(m)
            eps_r = jnp.where(chosen, eps_table[m][0], eps_r)
            eps_i = jnp.where(chosen, eps_table[m][1], eps_i)
        med_r = WAVE_SQUARED * (eps_r + SHIFT_IMAG * eps_i)
        med_i = WAVE_SQUARED * (eps_i - SHIFT_IMAG * eps_r)
        return label < MAT - 0.5, eps_r, eps_i, med_r, med_i

    def damped_inverse(inside, med_r, med_i, centre):
        diag = centre - med_r
        scale = jnp.where(inside, DAMPING / (diag * diag + med_i * med_i), 0.0)
        return diag * scale, med_i * scale

    def bcast(ref, at):
        return jnp.broadcast_to(ref[at], (8, nzc))

    def fill_start(x, carry):
        inside, eps_r, eps_i, med_r, med_i = media(lab[x])
        inv_r, inv_i = damped_inverse(inside, med_r, med_i, CENTRE)
        src_r = jnp.where(inside, SOURCE_GAIN * (eps_r - 1.0), 0.0)
        src_i = SOURCE_GAIN * eps_i
        tab[0, x] = inv_r * src_r - inv_i * src_i
        tab[1, x] = inv_r * src_i + inv_i * src_r
        tab[2, x] = inv_r * (1.0 / 30.0)
        tab[3, x] = inv_i * (1.0 / 30.0)
        tab[4, x] = (0.2 * (1.0 - DAMPING)) * src_r
        tab[5, x] = (0.2 * (1.0 - DAMPING)) * src_i
        for y in range(exty):
            wave_one, wave_two = wave[x, y, 0], wave[x, y, 1]
            for half in (0, 1):
                at = (x, pl.ds(2 * y + half, 1))
                it0[x, y, half] = bcast(tab, (0, *at)) * wave_one + bcast(tab, (1, *at)) * wave_two
        return carry

    lax.fori_loop(0, extx, fill_start, 0)

    def fill_coarse_table(i, carry):
        inside, _, _, med_r, med_i = media(lab[2 * i + LOW - 1])
        ctab[0, i], ctab[1, i] = damped_inverse(inside, med_r, med_i, COARSE_CENTRE)
        return carry

    lax.fori_loop(0, cx + 2, fill_coarse_table, 0)

    def times(real, imaginary, values):
        return real * values + imaginary * (sign * pltpu.roll(values, 4, 0))

    def sweep(x, carry):
        for y, even, odd in fine_neighbours(it0, x, range(1, exty - 1), first, last):
            for half, near in enumerate((even, odd)):
                at = (x, pl.ds(2 * y + half, 1))
                change = times(bcast(tab, (2, *at)), bcast(tab, (3, *at)), near)
                w[x, y, half] = (1.0 + 0.2 - DAMPING) * it0[x, y, half] + change
        return carry

    lax.fori_loop(1, extx - 1, sweep, 0)

    def iterate_out(x, carry):
        for y in range(sizey):
            for half in (0, 1):
                iterate_ref[x, y, half] = w[x + LOW, y + LOW, half] + DAMPING * it0[x + LOW, y + LOW, half]
        return carry

    lax.fori_loop(0, sizex, iterate_out, 0)

    def restrict(x, carry):
        in_x = jnp.where(jnp.logical_and(x == LOW + sizex, px == nx - 1), 0.0, 1.0 / 30.0)
        in_xy = jnp.where(py == ny - 1, 0.0, in_x)
        rows = []
        for y, even, odd in fine_neighbours(w, x, range(LOW, LOW + sizey + 1), first, last):
            wave_one, wave_two = wave[x, y, 0], wave[x, y, 1]
            scale = in_xy if y == LOW + sizey else in_x
            both = []
            for half, near in enumerate((even, odd)):
                at = (x, pl.ds(2 * y + half, 1))
                both.append(
                    bcast(tab, (4, *at)) * wave_one + bcast(tab, (5, *at)) * wave_two + scale * near
                )
            rows.append(both)
        for j in range(cy):
            even, odd = (
                (rows[2 * j][half] + rows[2 * j + 2][half]) + 2.0 * rows[2 * j + 1][half]
                for half in (0, 1)
            )
            yz[x - LOW, j] = (even + shift_down(even, last)) + 2.0 * odd
        return carry

    lax.fori_loop(LOW, LOW + sizex + 1, restrict, 0)

    def coarse_inverse(i, j):
        at = (i - 1, pl.ds(2 * (2 * (j - 2) + 1 + LOW) + 1, 1))
        return bcast(ctab, (0, *at)), bcast(ctab, (1, *at))

    def first_correction(i, carry):
        for j in range(cy):
            rhs = (yz[2 * i, j] + yz[2 * i + 2, j]) + 2.0 * yz[2 * i + 1, j]
            c0[i + 2, j + 2] = times(*coarse_inverse(i + 2, j + 2), rhs * (1.0 / 64.0))
        return carry

    lax.fori_loop(0, cx, first_correction, 0)
    sent_first = exchange(1, c0, (cx, cy), 2, 2, 1)
    finish(sent_first)

    def coarse_sweep(source, put, i_range, j_range):
        def body(i, carry):
            for j, near in coarse_neighbours(source, i, j_range, first, last):
                change = times(*coarse_inverse(i, j), near * (1.0 / 120.0))
                put(i, j, (1.0 - DAMPING) * source[i, j] + c0[i, j] + change)
            return carry

        lax.fori_loop(*i_range, body, 0)

    def into(ref, off):
        def put(i, j, values):
            ref[i - off, j - off] = values

        return put

    coarse_sweep(c0, into(c1, 0), (1, cx + 3), range(1, cy + 3))
    coarse_sweep(c1, into(c2, 0), (2, cx + 2), range(2, cy + 2))
    sent_third = exchange(2, c2, (cx, cy), 2, 1, 1)
    finish(sent_third)
    coarse_sweep(c2, into(corr_ref, 1), (1, cx + 2), range(1, cy + 2))
    for sent in (sent_labels, sent_first, sent_third):
        finish_sends(sent)


def prolong_kernel(iterate_ref, corr_ref, out_ref, flat):
    sizex, sizey = iterate_ref.shape[:2]
    nzc = iterate_ref.shape[-1]
    sizez = 2 * nzc
    lane = lax.broadcasted_iota(jnp.int32, (8, nzc), 1)
    first = lane == 0
    row = lax.broadcasted_iota(jnp.int32, (sizez, sizez), 0)
    col = lax.broadcasted_iota(jnp.int32, (sizez, sizez), 1)
    merge = jnp.where(col == jnp.where(row < nzc, 2 * row, 2 * (row - nzc) + 1), 1.0, 0.0).astype(jnp.bfloat16)

    for x in range(sizex):
        i = x // 2 + 1
        across = {}
        for j in range(sizey // 2 + 1):
            across[j] = corr_ref[i, j] if x % 2 else (corr_ref[i - 1, j] + corr_ref[i, j]) * 0.5
        rows = []
        for y in range(sizey):
            j = y // 2 + 1
            odd = across[j] if y % 2 else (across[j - 1] + across[j]) * 0.5
            even = (odd + shift_up(odd, first)) * 0.5
            rows.append(
                jnp.concatenate([iterate_ref[x, y, 0] + even, iterate_ref[x, y, 1] + odd], axis=1)
            )
        block = jnp.concatenate(rows, axis=0)
        top = block.astype(jnp.bfloat16)
        rest = block - top.astype(f32)
        mid = rest.astype(jnp.bfloat16)
        tail = (rest - mid.astype(f32)).astype(jnp.bfloat16)
        merged = (
            jnp.dot(tail, merge, preferred_element_type=f32)
            + jnp.dot(mid, merge, preferred_element_type=f32)
            + jnp.dot(top, merge, preferred_element_type=f32)
        )
        for half in (0, 1):
            flat[x, half] = merged[:, half * nzc : (half + 1) * nzc]
        for f in range(8):
            for half in (0, 1):
                out_ref[f // 4, f % 4, x, :, half * nzc : (half + 1) * nzc] = flat[
                    x, half, pl.ds(f, sizey, stride=8), :
                ]


def local(nx, ny, labels, eps_r, eps_i, angles, pick):
    sizex, sizey, sizez = labels.shape
    nzc = sizez // 2
    cx, cy = sizex // 2, sizey // 2
    extx, exty = sizex + LOW + HIGH, sizey + LOW + HIGH
    vmem = pl.BlockSpec(memory_space=pltpu.VMEM)
    smem = pl.BlockSpec(memory_space=pltpu.SMEM)
    iterate, corr = pl.pallas_call(
        functools.partial(cycle_kernel, nx, ny),
        out_shape=(
            jax.ShapeDtypeStruct((sizex, sizey, 2, 8, nzc), f32),
            jax.ShapeDtypeStruct((cx + 1, cy + 1, 8, nzc), f32),
        ),
        in_specs=[vmem, smem, smem, smem, smem],
        out_specs=(vmem, vmem),
        scratch_shapes=[
            pltpu.VMEM((extx, 2 * exty, nzc), f32),
            pltpu.VMEM((6, extx, 2 * exty, nzc), f32),
            pltpu.VMEM((2, cx + 2, 2 * exty, nzc), f32),
            pltpu.VMEM((extx + exty, 2, 8, nzc), f32),
            pltpu.VMEM((extx, exty, 2, 8, nzc), f32),
            pltpu.VMEM((extx, exty, 2, 8, nzc), f32),
            pltpu.VMEM((extx, exty, 2, 8, nzc), f32),
            pltpu.VMEM((sizex + 1, cy, 8, nzc), f32),
            pltpu.VMEM((cx + 4, cy + 4, 8, nzc), f32),
            pltpu.VMEM((cx + 4, cy + 4, 8, nzc), f32),
            pltpu.VMEM((cx + 4, cy + 4, 8, nzc), f32),
            pltpu.SemaphoreType.DMA((3, len(DIRS))),
            pltpu.SemaphoreType.DMA((3, len(DIRS))),
        ],
        compiler_params=pltpu.CompilerParams(
            collective_id=0, has_side_effects=True, vmem_limit_bytes=24 * 2**20
        ),
    )(labels, eps_r, eps_i, angles, pick)
    return pl.pallas_call(
        prolong_kernel,
        out_shape=jax.ShapeDtypeStruct((2, 4, sizex, sizey, sizez), f32),
        in_specs=[vmem, vmem],
        out_specs=vmem,
        scratch_shapes=[pltpu.VMEM((sizex, 2, 8 * sizey, nzc), f32)],
        compiler_params=pltpu.CompilerParams(vmem_limit_bytes=16 * 2**20),
    )(iterate, corr)


def solution(mesh):
    return jax.shard_map(
        functools.partial(local, mesh.shape["gx"], mesh.shape["gy"]),
        mesh=mesh,
        in_specs=(P("gx", "gy", None), P(), P(), P(), P()),
        out_specs=P(None, None, "gx", "gy", None),
        check_vma=False,
    )
```

```python
import functools

import jax
import jax.numpy as jnp
from jax import lax
from jax.experimental import pallas as pl
from jax.experimental.pallas import tpu as pltpu
from jax.sharding import PartitionSpec as P

MAT = 8
DAMPING = 0.8
WAVE_SQUARED = 0.1
SHIFT_IMAG = 0.5
SOURCE_GAIN = 4.0
CENTRE = 128.0 / 30.0
COARSE_CENTRE = 128.0 / 120.0
LOW, HIGH = 2, 3
DIRS = [(dx, dy) for dx in (-1, 0, 1) for dy in (-1, 0, 1) if (dx, dy) != (0, 0)]
f32 = jnp.float32


def windows(step, size, low, high):
    if step == 0:
        return low, low, size
    if step > 0:
        return size, 0, low
    return low, low + size, high


def shift_up(values, first):
    return jnp.where(first, 0.0, pltpu.roll(values, 1, 1))


def shift_down(values, last):
    return jnp.where(last, 0.0, pltpu.roll(values, values.shape[1] - 1, 1))


def plane_sums(centre, ends, y):
    side = ends[y] + (centre[y - 1] + centre[y + 1])
    diag = ends[y - 1] + ends[y + 1]
    return 14.0 * side + 3.0 * diag, 14.0 * centre[y] + (3.0 * side + diag)


def fine_neighbours(buf, x, rows, first, last):
    span = range(rows[0] - 1, rows[-1] + 2)
    halves = []
    for half in (0, 1):
        centre = {y: buf[x, y, half] for y in span}
        ends = {y: buf[x - 1, y, half] + buf[x + 1, y, half] for y in span}
        halves.append([plane_sums(centre, ends, y) for y in rows])
    for i, y in enumerate(rows):
        (in_even, out_even), (in_odd, out_odd) = halves[0][i], halves[1][i]
        yield (
            y,
            in_even + (out_odd + shift_up(out_odd, first)),
            in_odd + (out_even + shift_down(out_even, last)),
        )


def coarse_neighbours(buf, x, rows, first, last):
    span = range(rows[0] - 1, rows[-1] + 2)
    centre = {y: buf[x, y] for y in span}
    ends = {y: buf[x - 1, y] + buf[x + 1, y] for y in span}
    for y in rows:
        inner, outer = plane_sums(centre, ends, y)
        yield y, inner + (shift_up(outer, first) + shift_down(outer, last))


def cycle_kernel(
    nx, ny,
    labels_hbm, eps_r_hbm, eps_i_hbm, angles_hbm, pick_hbm,
    iterate_ref, corr_ref,
    labels_ref, eps_r_ref, eps_i_ref, angles_ref, pick_ref, load_sems,
    lab, tab, ctab, ewave, wave, it0, w, yz, c0, c1, c2,
    send_sems, recv_sems, plane_sends, plane_recvs, iterate, store_sem,
):
    loads = []
    for k, (source, target) in enumerate((
        (labels_hbm, labels_ref),
        (pick_hbm, pick_ref),
        (angles_hbm, angles_ref),
        (eps_r_hbm, eps_r_ref),
        (eps_i_hbm, eps_i_ref),
    )):
        loads.append(pltpu.make_async_copy(source, target, load_sems.at[k]))
        loads[-1].start()
    sizex, sizey, sizez = labels_ref.shape
    nzc = sizez // 2
    cx, cy = sizex // 2, sizey // 2
    extx, exty = sizex + LOW + HIGH, sizey + LOW + HIGH
    px, py = lax.axis_index("gx"), lax.axis_index("gy")

    def there(dx, dy):
        ok = None
        for step, pos, count in ((dx, px, nx), (dy, py, ny)):
            if step:
                one = (pos > 0) if step < 0 else (pos < count - 1)
                ok = one if ok is None else jnp.logical_and(ok, one)
        return ok

    lab[...] = jnp.full(lab.shape, float(MAT), f32)
    c0[...] = jnp.zeros(c0.shape, f32)
    c2[...] = jnp.zeros(c2.shape, f32)
    barrier = pltpu.get_barrier_semaphore()
    for dx, dy in DIRS:
        @pl.when(there(dx, dy))
        def _():
            pl.semaphore_signal(
                barrier, inc=1, device_id=(px + dx, py + dy), device_id_type=pl.DeviceIdType.MESH
            )

    row = lax.broadcasted_iota(jnp.int32, (sizez, sizez), 0)
    col = lax.broadcasted_iota(jnp.int32, (sizez, sizez), 1)
    split = jnp.where(row == jnp.where(col < nzc, 2 * col, 2 * (col - nzc) + 1), 1.0, 0.0).astype(jnp.bfloat16)
    loads[0].wait()
    mine = labels_ref[...].astype(f32).reshape(sizex * sizey, sizez).astype(jnp.bfloat16)
    mine = jnp.dot(mine, split, preferred_element_type=f32)
    for x in range(sizex):
        for half in (0, 1):
            lab[x + LOW, pl.ds(2 * LOW + half, sizey, stride=2), :] = mine[
                x * sizey : (x + 1) * sizey, half * nzc : (half + 1) * nzc
            ]

    def exchange(phase, buf, sizes, low, high, fold):
        copies = []
        for d, (dx, dy) in enumerate(DIRS):
            fx, tx, lx = windows(dx, sizes[0], low, high)
            fy, ty, ly = windows(dy, sizes[1], low, high)
            out = pltpu.make_async_remote_copy(
                src_ref=buf.at[pl.ds(fx, lx), pl.ds(fold * fy, fold * ly)],
                dst_ref=buf.at[pl.ds(tx, lx), pl.ds(fold * ty, fold * ly)],
                send_sem=send_sems.at[phase, d],
                recv_sem=recv_sems.at[phase, d],
                device_id=(px + dx, py + dy),
                device_id_type=pl.DeviceIdType.MESH,
            )
            copies.append(out)
            pl.when(there(dx, dy))(out.start)
        return copies

    def finish(copies):
        for (dx, dy), copy in zip(DIRS, copies):
            pl.when(there(-dx, -dy))(copy.wait_recv)

    def finish_sends(copies):
        for (dx, dy), copy in zip(DIRS, copies):
            pl.when(there(dx, dy))(copy.wait_send)

    one = jnp.int32(1)
    besides_x = jnp.where(px > 0, one, 0) + jnp.where(px < nx - 1, one, 0)
    besides_y = jnp.where(py > 0, one, 0) + jnp.where(py < ny - 1, one, 0)
    pl.semaphore_wait(barrier, (besides_x + 1) * (besides_y + 1) - 1)
    sent_labels = exchange(0, lab, (sizex, sizey), LOW, HIGH, 2)

    lane = lax.broadcasted_iota(jnp.int32, (8, nzc), 1)
    field = lax.broadcasted_iota(jnp.int32, (8, nzc), 0)
    first, last = lane == 0, lane == nzc - 1
    imag = field >= 4
    sign = jnp.where(imag, 1.0, -1.0)
    column = field % 4
    incidence = jnp.zeros((8, nzc), f32)
    for load in loads[1:]:
        load.wait()
    for c in range(4):
        incidence = jnp.where(column == c, angles_ref[pick_ref[c]], incidence)
    wavenumber = jnp.sqrt(jnp.full((8, nzc), WAVE_SQUARED, f32))
    on_x = lane < nzc // 2
    place = jnp.where(on_x, px * sizex - LOW + lane, py * sizey - LOW + lane - nzc // 2).astype(f32)
    arg = wavenumber * jnp.where(on_x, jnp.cos(incidence), jnp.sin(incidence)) * place
    cos_all, sin_all = jnp.cos(arg), jnp.sin(arg)
    one_all = jnp.where(imag, sin_all, cos_all)
    two_all = jnp.where(imag, cos_all, -sin_all)
    spread = lambda values, at: jnp.broadcast_to(values[:, at : at + 1], (8, nzc))
    for x in range(extx):
        ewave[x, 0] = spread(one_all, x)
        ewave[x, 1] = spread(two_all, x)
    along_y = [
        (spread(cos_all, nzc // 2 + y), spread(sin_all, nzc // 2 + y)) for y in range(exty)
    ]
    for y in range(exty):
        ewave[extx + y, 0], ewave[extx + y, 1] = along_y[y]

    def fill_wave(x, carry):
        wave_one, wave_two = ewave[x, 0], ewave[x, 1]
        for y in range(exty):
            cos_y, sin_y = ewave[extx + y, 0], ewave[extx + y, 1]
            wave[x, y, 0] = cos_y * wave_one + sin_y * wave_two
            wave[x, y, 1] = cos_y * wave_two - sin_y * wave_one
        return carry

    lax.fori_loop(0, extx, fill_wave, 0)
    eps_table = [(eps_r_ref[m], eps_i_ref[m]) for m in range(MAT)]
    finish(sent_labels)

    def media(label):
        eps_r = jnp.zeros(label.shape, f32)
        eps_i = jnp.zeros(label.shape, f32)
        for m in range(MAT):
            chosen = label == float(m)
            eps_r = jnp.where(chosen, eps_table[m][0], eps_r)
            eps_i = jnp.where(chosen, eps_table[m][1], eps_i)
        med_r = WAVE_SQUARED * (eps_r + SHIFT_IMAG * eps_i)
        med_i = WAVE_SQUARED * (eps_i - SHIFT_IMAG * eps_r)
        return label < MAT - 0.5, eps_r, eps_i, med_r, med_i

    def damped_inverse(inside, med_r, med_i, centre):
        diag = centre - med_r
        scale = jnp.where(inside, DAMPING / (diag * diag + med_i * med_i), 0.0)
        return diag * scale, med_i * scale

    def bcast(ref, at):
        return jnp.broadcast_to(ref[at], (8, nzc))

    def fill_start(x, carry):
        inside, eps_r, eps_i, med_r, med_i = media(lab[x])
        inv_r, inv_i = damped_inverse(inside, med_r, med_i, CENTRE)
        src_r = jnp.where(inside, SOURCE_GAIN * (eps_r - 1.0), 0.0)
        src_i = SOURCE_GAIN * eps_i
        tab[0, x] = inv_r * src_r - inv_i * src_i
        tab[1, x] = inv_r * src_i + inv_i * src_r
        tab[2, x] = inv_r * (1.0 / 30.0)
        tab[3, x] = inv_i * (1.0 / 30.0)
        tab[4, x] = (0.2 * (1.0 - DAMPING)) * src_r
        tab[5, x] = (0.2 * (1.0 - DAMPING)) * src_i
        for y in range(exty):
            wave_one, wave_two = wave[x, y, 0], wave[x, y, 1]
            for half in (0, 1):
                at = (x, pl.ds(2 * y + half, 1))
                it0[x, y, half] = bcast(tab, (0, *at)) * wave_one + bcast(tab, (1, *at)) * wave_two
        return carry


    def fill_coarse_table(i, carry):
        inside, _, _, med_r, med_i = media(lab[2 * i + LOW - 1])
        ctab[0, i], ctab[1, i] = damped_inverse(inside, med_r, med_i, COARSE_CENTRE)
        return carry

    def times(real, imaginary, values):
        return real * values + imaginary * (sign * pltpu.roll(values, 4, 0))

    def sweep(x, carry):
        for y, even, odd in fine_neighbours(it0, x, range(1, exty - 1), first, last):
            for half, near in enumerate((even, odd)):
                at = (x, pl.ds(2 * y + half, 1))
                change = times(bcast(tab, (2, *at)), bcast(tab, (3, *at)), near)
                w[x, y, half] = (1.0 + 0.2 - DAMPING) * it0[x, y, half] + change
        return carry

    def restrict(x, carry):
        in_x = jnp.where(jnp.logical_and(x == LOW + sizex, px == nx - 1), 0.0, 1.0 / 30.0)
        in_xy = jnp.where(py == ny - 1, 0.0, in_x)
        rows = []
        for y, even, odd in fine_neighbours(w, x, range(LOW, LOW + sizey + 1), first, last):
            wave_one, wave_two = wave[x, y, 0], wave[x, y, 1]
            scale = in_xy if y == LOW + sizey else in_x
            both = []
            for half, near in enumerate((even, odd)):
                at = (x, pl.ds(2 * y + half, 1))
                both.append(
                    bcast(tab, (4, *at)) * wave_one + bcast(tab, (5, *at)) * wave_two + scale * near
                )
            rows.append(both)
        for j in range(cy):
            even, odd = (
                (rows[2 * j][half] + rows[2 * j + 2][half]) + 2.0 * rows[2 * j + 1][half]
                for half in (0, 1)
            )
            yz[x - LOW, j] = (even + shift_down(even, last)) + 2.0 * odd
        return carry

    def coarse_inverse(i, j):
        at = (i - 1, pl.ds(2 * (2 * (j - 2) + 1 + LOW) + 1, 1))
        return bcast(ctab, (0, *at)), bcast(ctab, (1, *at))

    def first_correction(i, carry):
        for j in range(cy):
            rhs = (yz[2 * i, j] + yz[2 * i + 2, j]) + 2.0 * yz[2 * i + 1, j]
            c0[i + 2, j + 2] = times(*coarse_inverse(i + 2, j + 2), rhs * (1.0 / 64.0))
        return carry

    def send_plane(i):
        copies = []
        for dx in (-1, 1, 0):
            if (dx < 0 and i >= 2) or (dx > 0 and i < cx - 2):
                continue
            to = i + 2 - dx * cx
            for dy in (-1, 1, 0):
                if dx == 0 and dy == 0:
                    continue
                fy, ty, ly = windows(dy, cy, 2, 2)
                d = DIRS.index((dx, dy))
                copy = pltpu.make_async_remote_copy(
                    src_ref=c0.at[i + 2, pl.ds(fy, ly)],
                    dst_ref=c0.at[to, pl.ds(ty, ly)],
                    send_sem=plane_sends.at[i, d],
                    recv_sem=plane_recvs.at[i, d],
                    device_id=(px + dx, py + dy),
                    device_id_type=pl.DeviceIdType.MESH,
                )
                pl.when(there(dx, dy))(copy.start)
                copies.append(((dx, dy), copy))
        return copies

    lax.fori_loop(0, cx + 2, fill_coarse_table, 0)
    sent_planes = []
    for i in range(cx):
        upto = 2 * i + 7
        lax.fori_loop(upto - 2 if i else 0, upto, fill_start, 0)
        lax.fori_loop(upto - 3 if i else 1, upto - 1, sweep, 0)
        lax.fori_loop(upto - 4 if i else LOW, upto - 2, restrict, 0)
        first_correction(i, 0)
        sent_planes += send_plane(i)

    def iterate_out(x, carry):
        for y in range(sizey):
            for half in (0, 1):
                iterate[x, y, half] = w[x + LOW, y + LOW, half] + DAMPING * it0[x + LOW, y + LOW, half]
        return carry

    lax.fori_loop(0, sizex, iterate_out, 0)
    store = pltpu.make_async_copy(iterate, iterate_ref, store_sem)
    store.start()
    for (dx, dy), copy in sent_planes:
        pl.when(there(-dx, -dy))(copy.wait_recv)

    def coarse_sweep(source, put, i_range, j_range):
        def body(i, carry):
            for j, near in coarse_neighbours(source, i, j_range, first, last):
                change = times(*coarse_inverse(i, j), near * (1.0 / 120.0))
                put(i, j, (1.0 - DAMPING) * source[i, j] + c0[i, j] + change)
            return carry

        lax.fori_loop(*i_range, body, 0)

    def into(ref, off):
        def put(i, j, values):
            ref[i - off, j - off] = values

        return put

    coarse_sweep(c0, into(c1, 0), (1, cx + 3), range(1, cy + 3))
    coarse_sweep(c1, into(c2, 0), (2, cx + 2), range(2, cy + 2))
    sent_third = exchange(1, c2, (cx, cy), 2, 1, 1)
    finish(sent_third)
    coarse_sweep(c2, into(corr_ref, 1), (1, cx + 2), range(1, cy + 2))
    for sent in (sent_labels, sent_third):
        finish_sends(sent)
    for (dx, dy), copy in sent_planes:
        pl.when(there(dx, dy))(copy.wait_send)
    store.wait()


def prolong_kernel(iterate_hbm, corr_hbm, out_hbm, iterate_ref, corr_ref, out_ref, flat, load_sems, store_sems):
    sizex, sizey = iterate_ref.shape[:2]
    loads = [pltpu.make_async_copy(corr_hbm, corr_ref, load_sems.at[sizex])]
    for x in range(sizex):
        loads.append(pltpu.make_async_copy(iterate_hbm.at[x], iterate_ref.at[x], load_sems.at[x]))
    for load in loads:
        load.start()
    stores = []
    nzc = iterate_ref.shape[-1]
    sizez = 2 * nzc
    lane = lax.broadcasted_iota(jnp.int32, (8, nzc), 1)
    first = lane == 0
    row = lax.broadcasted_iota(jnp.int32, (sizez, sizez), 0)
    col = lax.broadcasted_iota(jnp.int32, (sizez, sizez), 1)
    merge = jnp.where(col == jnp.where(row < nzc, 2 * row, 2 * (row - nzc) + 1), 1.0, 0.0).astype(jnp.bfloat16)

    loads[0].wait()
    for x in range(sizex):
        loads[x + 1].wait()
        i = x // 2 + 1
        across = {}
        for j in range(sizey // 2 + 1):
            across[j] = corr_ref[i, j] if x % 2 else (corr_ref[i - 1, j] + corr_ref[i, j]) * 0.5
        rows = []
        for y in range(sizey):
            j = y // 2 + 1
            odd = across[j] if y % 2 else (across[j - 1] + across[j]) * 0.5
            even = (odd + shift_up(odd, first)) * 0.5
            rows.append(
                jnp.concatenate([iterate_ref[x, y, 0] + even, iterate_ref[x, y, 1] + odd], axis=1)
            )
        block = jnp.concatenate(rows, axis=0)
        top = block.astype(jnp.bfloat16)
        rest = block - top.astype(f32)
        mid = rest.astype(jnp.bfloat16)
        tail = (rest - mid.astype(f32)).astype(jnp.bfloat16)
        merged = (
            jnp.dot(tail, merge, preferred_element_type=f32)
            + jnp.dot(mid, merge, preferred_element_type=f32)
            + jnp.dot(top, merge, preferred_element_type=f32)
        )
        for half in (0, 1):
            flat[x, half] = merged[:, half * nzc : (half + 1) * nzc]
        for f in range(8):
            for half in (0, 1):
                out_ref[x, f // 4, f % 4, :, half * nzc : (half + 1) * nzc] = flat[
                    x, half, pl.ds(f, sizey, stride=8), :
                ]
        stores.append(pltpu.make_async_copy(out_ref.at[x], out_hbm.at[:, :, x], store_sems.at[x]))
        stores[-1].start()
    for store in stores:
        store.wait()


def local(nx, ny, labels, eps_r, eps_i, angles, pick):
    sizex, sizey, sizez = labels.shape
    nzc = sizez // 2
    cx, cy = sizex // 2, sizey // 2
    extx, exty = sizex + LOW + HIGH, sizey + LOW + HIGH
    vmem = pl.BlockSpec(memory_space=pltpu.VMEM)
    hbm = pl.BlockSpec(memory_space=pltpu.HBM)
    iterate, corr = pl.pallas_call(
        functools.partial(cycle_kernel, nx, ny),
        out_shape=(
            jax.ShapeDtypeStruct((sizex, sizey, 2, 8, nzc), f32),
            jax.ShapeDtypeStruct((cx + 1, cy + 1, 8, nzc), f32),
        ),
        in_specs=[hbm] * 5,
        out_specs=(hbm, vmem),
        scratch_shapes=[
            pltpu.VMEM(labels.shape, jnp.int32),
            pltpu.SMEM(eps_r.shape, f32),
            pltpu.SMEM(eps_i.shape, f32),
            pltpu.SMEM(angles.shape, f32),
            pltpu.SMEM(pick.shape, jnp.int32),
            pltpu.SemaphoreType.DMA((5,)),
            pltpu.VMEM((extx, 2 * exty, nzc), f32),
            pltpu.VMEM((6, extx, 2 * exty, nzc), f32),
            pltpu.VMEM((2, cx + 2, 2 * exty, nzc), f32),
            pltpu.VMEM((extx + exty, 2, 8, nzc), f32),
            pltpu.VMEM((extx, exty, 2, 8, nzc), f32),
            pltpu.VMEM((extx, exty, 2, 8, nzc), f32),
            pltpu.VMEM((extx, exty, 2, 8, nzc), f32),
            pltpu.VMEM((sizex + 1, cy, 8, nzc), f32),
            pltpu.VMEM((cx + 4, cy + 4, 8, nzc), f32),
            pltpu.VMEM((cx + 4, cy + 4, 8, nzc), f32),
            pltpu.VMEM((cx + 4, cy + 4, 8, nzc), f32),
            pltpu.SemaphoreType.DMA((2, len(DIRS))),
            pltpu.SemaphoreType.DMA((2, len(DIRS))),
            pltpu.SemaphoreType.DMA((cx, len(DIRS))),
            pltpu.SemaphoreType.DMA((cx, len(DIRS))),
            pltpu.VMEM((sizex, sizey, 2, 8, nzc), f32),
            pltpu.SemaphoreType.DMA,
        ],
        compiler_params=pltpu.CompilerParams(
            collective_id=0, has_side_effects=True, vmem_limit_bytes=60 * 2**20
        ),
    )(labels, eps_r, eps_i, angles, pick)
    return pl.pallas_call(
        prolong_kernel,
        out_shape=jax.ShapeDtypeStruct((2, 4, sizex, sizey, sizez), f32),
        in_specs=[hbm, hbm],
        out_specs=hbm,
        scratch_shapes=[
            pltpu.VMEM((sizex, sizey, 2, 8, nzc), f32),
            pltpu.VMEM((cx + 1, cy + 1, 8, nzc), f32),
            pltpu.VMEM((sizex, 2, 4, sizey, sizez), f32),
            pltpu.VMEM((sizex, 2, 8 * sizey, nzc), f32),
            pltpu.SemaphoreType.DMA((sizex + 1,)),
            pltpu.SemaphoreType.DMA((sizex,)),
        ],
        compiler_params=pltpu.CompilerParams(vmem_limit_bytes=60 * 2**20),
    )(iterate, corr)


def solution(mesh):
    return jax.shard_map(
        functools.partial(local, mesh.shape["gx"], mesh.shape["gy"]),
        mesh=mesh,
        in_specs=(P("gx", "gy", None), P(), P(), P(), P()),
        out_specs=P(None, None, "gx", "gy", None),
        check_vma=False,
    )
```

```python
import functools

import jax
import jax.numpy as jnp
from jax import lax
from jax.experimental import pallas as pl
from jax.experimental.pallas import tpu as pltpu
from jax.sharding import PartitionSpec as P

MAT = 8
DAMPING = 0.8
WAVE_SQUARED = 0.1
SHIFT_IMAG = 0.5
SOURCE_GAIN = 4.0
CENTRE = 128.0 / 30.0
COARSE_CENTRE = 128.0 / 120.0
LOW, HIGH = 2, 3
DIRS = [(-1, 0), (1, 0), (-1, -1), (1, 1), (-1, 1), (1, -1), (0, -1), (0, 1)]
f32 = jnp.float32


def windows(step, size, low, high):
    if step == 0:
        return low, low, size
    if step > 0:
        return size, 0, low
    return low, low + size, high


def shift_up(values, first):
    return jnp.where(first, 0.0, pltpu.roll(values, 1, 1))


def shift_down(values, last):
    return jnp.where(last, 0.0, pltpu.roll(values, values.shape[1] - 1, 1))


def plane_sums(centre, ends, y):
    side = ends[y] + (centre[y - 1] + centre[y + 1])
    diag = ends[y - 1] + ends[y + 1]
    return 14.0 * side + 3.0 * diag, 14.0 * centre[y] + (3.0 * side + diag)


def fine_neighbours(buf, x, rows, first, last):
    span = range(rows[0] - 1, rows[-1] + 2)
    halves = []
    for half in (0, 1):
        centre = {y: buf[x, y, half] for y in span}
        ends = {y: buf[x - 1, y, half] + buf[x + 1, y, half] for y in span}
        halves.append([plane_sums(centre, ends, y) for y in rows])
    for i, y in enumerate(rows):
        (in_even, out_even), (in_odd, out_odd) = halves[0][i], halves[1][i]
        yield (
            y,
            in_even + (out_odd + shift_up(out_odd, first)),
            in_odd + (out_even + shift_down(out_even, last)),
        )


def coarse_neighbours(buf, x, rows, first, last):
    span = range(rows[0] - 1, rows[-1] + 2)
    centre = {y: buf[x, y] for y in span}
    ends = {y: buf[x - 1, y] + buf[x + 1, y] for y in span}
    for y in rows:
        inner, outer = plane_sums(centre, ends, y)
        yield y, inner + (shift_up(outer, first) + shift_down(outer, last))


def cycle_kernel(
    nx, ny,
    labels_hbm, eps_r_hbm, eps_i_hbm, angles_hbm, pick_hbm,
    iterate_ref, corr_ref,
    labels_ref, eps_r_ref, eps_i_ref, angles_ref, pick_ref, load_sems,
    lab, tab, ctab, ewave, wave, it0, w, yz, c0, c1, c2,
    send_sems, recv_sems, plane_sends, plane_recvs,
):
    loads = []
    for k, (source, target) in enumerate((
        (labels_hbm, labels_ref),
        (pick_hbm, pick_ref),
        (angles_hbm, angles_ref),
        (eps_r_hbm, eps_r_ref),
        (eps_i_hbm, eps_i_ref),
    )):
        loads.append(pltpu.make_async_copy(source, target, load_sems.at[k]))
        loads[-1].start()
    sizex, sizey, sizez = labels_ref.shape
    nzc = sizez // 2
    cx, cy = sizex // 2, sizey // 2
    extx, exty = sizex + LOW + HIGH, sizey + LOW + HIGH
    px, py = lax.axis_index("gx"), lax.axis_index("gy")

    def there(dx, dy):
        ok = None
        for step, pos, count in ((dx, px, nx), (dy, py, ny)):
            if step:
                one = (pos > 0) if step < 0 else (pos < count - 1)
                ok = one if ok is None else jnp.logical_and(ok, one)
        return ok

    lab[...] = jnp.full(lab.shape, float(MAT), f32)
    c0[...] = jnp.zeros(c0.shape, f32)
    c2[...] = jnp.zeros(c2.shape, f32)
    barrier = pltpu.get_barrier_semaphore()
    for dx, dy in DIRS:
        @pl.when(there(dx, dy))
        def _():
            pl.semaphore_signal(
                barrier, inc=1, device_id=(px + dx, py + dy), device_id_type=pl.DeviceIdType.MESH
            )

    row = lax.broadcasted_iota(jnp.int32, (sizez, sizez), 0)
    col = lax.broadcasted_iota(jnp.int32, (sizez, sizez), 1)
    split = jnp.where(row == jnp.where(col < nzc, 2 * col, 2 * (col - nzc) + 1), 1.0, 0.0).astype(jnp.bfloat16)
    loads[0].wait()
    mine = labels_ref[...].astype(f32).reshape(sizex * sizey, sizez).astype(jnp.bfloat16)
    mine = jnp.dot(mine, split, preferred_element_type=f32)
    for x in range(sizex):
        for half in (0, 1):
            lab[x + LOW, pl.ds(2 * LOW + half, sizey, stride=2), :] = mine[
                x * sizey : (x + 1) * sizey, half * nzc : (half + 1) * nzc
            ]

    def exchange(phase, buf, sizes, low, high, fold):
        copies = []
        for d, (dx, dy) in enumerate(DIRS):
            fx, tx, lx = windows(dx, sizes[0], low, high)
            fy, ty, ly = windows(dy, sizes[1], low, high)
            out = pltpu.make_async_remote_copy(
                src_ref=buf.at[pl.ds(fx, lx), pl.ds(fold * fy, fold * ly)],
                dst_ref=buf.at[pl.ds(tx, lx), pl.ds(fold * ty, fold * ly)],
                send_sem=send_sems.at[phase, d],
                recv_sem=recv_sems.at[phase, d],
                device_id=(px + dx, py + dy),
                device_id_type=pl.DeviceIdType.MESH,
            )
            copies.append(out)
            pl.when(there(dx, dy))(out.start)
        return copies

    def finish(copies):
        for (dx, dy), copy in zip(DIRS, copies):
            pl.when(there(-dx, -dy))(copy.wait_recv)

    def finish_sends(copies):
        for (dx, dy), copy in zip(DIRS, copies):
            pl.when(there(dx, dy))(copy.wait_send)

    one = jnp.int32(1)
    besides_x = jnp.where(px > 0, one, 0) + jnp.where(px < nx - 1, one, 0)
    besides_y = jnp.where(py > 0, one, 0) + jnp.where(py < ny - 1, one, 0)
    pl.semaphore_wait(barrier, (besides_x + 1) * (besides_y + 1) - 1)
    sent_labels = exchange(0, lab, (sizex, sizey), LOW, HIGH, 2)

    lane = lax.broadcasted_iota(jnp.int32, (8, nzc), 1)
    field = lax.broadcasted_iota(jnp.int32, (8, nzc), 0)
    first, last = lane == 0, lane == nzc - 1
    imag = field >= 4
    sign = jnp.where(imag, 1.0, -1.0)
    column = field % 4
    incidence = jnp.zeros((8, nzc), f32)
    for load in loads[1:]:
        load.wait()
    for c in range(4):
        incidence = jnp.where(column == c, angles_ref[pick_ref[c]], incidence)
    wavenumber = jnp.sqrt(jnp.full((8, nzc), WAVE_SQUARED, f32))
    on_x = lane < nzc // 2
    place = jnp.where(on_x, px * sizex - LOW + lane, py * sizey - LOW + lane - nzc // 2).astype(f32)
    arg = wavenumber * jnp.where(on_x, jnp.cos(incidence), jnp.sin(incidence)) * place
    cos_all, sin_all = jnp.cos(arg), jnp.sin(arg)
    one_all = jnp.where(imag, sin_all, cos_all)
    two_all = jnp.where(imag, cos_all, -sin_all)
    spread = lambda values, at: jnp.broadcast_to(values[:, at : at + 1], (8, nzc))
    for x in range(extx):
        ewave[x, 0] = spread(one_all, x)
        ewave[x, 1] = spread(two_all, x)
    along_y = [
        (spread(cos_all, nzc // 2 + y), spread(sin_all, nzc // 2 + y)) for y in range(exty)
    ]
    for y in range(exty):
        ewave[extx + y, 0], ewave[extx + y, 1] = along_y[y]

    def fill_wave(x, carry):
        wave_one, wave_two = ewave[x, 0], ewave[x, 1]
        for y in range(exty):
            cos_y, sin_y = ewave[extx + y, 0], ewave[extx + y, 1]
            wave[x, y, 0] = cos_y * wave_one + sin_y * wave_two
            wave[x, y, 1] = cos_y * wave_two - sin_y * wave_one
        return carry

    lax.fori_loop(0, extx, fill_wave, 0)
    eps_table = [(eps_r_ref[m], eps_i_ref[m]) for m in range(MAT)]
    finish(sent_labels)

    def media(label):
        eps_r = jnp.zeros(label.shape, f32)
        eps_i = jnp.zeros(label.shape, f32)
        for m in range(MAT):
            chosen = label == float(m)
            eps_r = jnp.where(chosen, eps_table[m][0], eps_r)
            eps_i = jnp.where(chosen, eps_table[m][1], eps_i)
        med_r = WAVE_SQUARED * (eps_r + SHIFT_IMAG * eps_i)
        med_i = WAVE_SQUARED * (eps_i - SHIFT_IMAG * eps_r)
        return label < MAT - 0.5, eps_r, eps_i, med_r, med_i

    def damped_inverse(inside, med_r, med_i, centre):
        diag = centre - med_r
        scale = jnp.where(inside, DAMPING / (diag * diag + med_i * med_i), 0.0)
        return diag * scale, med_i * scale

    def bcast(ref, at):
        return jnp.broadcast_to(ref[at], (8, nzc))

    def fill_start(x, carry):
        inside, eps_r, eps_i, med_r, med_i = media(lab[x])
        inv_r, inv_i = damped_inverse(inside, med_r, med_i, CENTRE)
        src_r = jnp.where(inside, SOURCE_GAIN * (eps_r - 1.0), 0.0)
        src_i = SOURCE_GAIN * eps_i
        tab[0, x] = inv_r * src_r - inv_i * src_i
        tab[1, x] = inv_r * src_i + inv_i * src_r
        tab[2, x] = inv_r * (1.0 / 30.0)
        tab[3, x] = inv_i * (1.0 / 30.0)
        tab[4, x] = (0.2 * (1.0 - DAMPING)) * src_r
        tab[5, x] = (0.2 * (1.0 - DAMPING)) * src_i
        for y in range(exty):
            wave_one, wave_two = wave[x, y, 0], wave[x, y, 1]
            for half in (0, 1):
                at = (x, pl.ds(2 * y + half, 1))
                it0[x, y, half] = bcast(tab, (0, *at)) * wave_one + bcast(tab, (1, *at)) * wave_two
        return carry


    def fill_coarse_table(i, carry):
        inside, _, _, med_r, med_i = media(lab[2 * i + LOW - 1])
        ctab[0, i], ctab[1, i] = damped_inverse(inside, med_r, med_i, COARSE_CENTRE)
        return carry

    def times(real, imaginary, values):
        return real * values + imaginary * (sign * pltpu.roll(values, 4, 0))

    def sweep(x, carry):
        for y, even, odd in fine_neighbours(it0, x, range(1, exty - 1), first, last):
            for half, near in enumerate((even, odd)):
                at = (x, pl.ds(2 * y + half, 1))
                change = times(bcast(tab, (2, *at)), bcast(tab, (3, *at)), near)
                w[x, y, half] = (1.0 + 0.2 - DAMPING) * it0[x, y, half] + change
        return carry

    def restrict(x, carry):
        in_x = jnp.where(jnp.logical_and(x == LOW + sizex, px == nx - 1), 0.0, 1.0 / 30.0)
        in_xy = jnp.where(py == ny - 1, 0.0, in_x)
        rows = []
        for y, even, odd in fine_neighbours(w, x, range(LOW, LOW + sizey + 1), first, last):
            wave_one, wave_two = wave[x, y, 0], wave[x, y, 1]
            scale = in_xy if y == LOW + sizey else in_x
            both = []
            for half, near in enumerate((even, odd)):
                at = (x, pl.ds(2 * y + half, 1))
                both.append(
                    bcast(tab, (4, *at)) * wave_one + bcast(tab, (5, *at)) * wave_two + scale * near
                )
            rows.append(both)
        for j in range(cy):
            even, odd = (
                (rows[2 * j][half] + rows[2 * j + 2][half]) + 2.0 * rows[2 * j + 1][half]
                for half in (0, 1)
            )
            yz[x - LOW, j] = (even + shift_down(even, last)) + 2.0 * odd
        return carry

    def coarse_inverse(i, j):
        at = (i - 1, pl.ds(2 * (2 * (j - 2) + 1 + LOW) + 1, 1))
        return bcast(ctab, (0, *at)), bcast(ctab, (1, *at))

    def first_correction(i, carry):
        for j in range(cy):
            rhs = (yz[2 * i, j] + yz[2 * i + 2, j]) + 2.0 * yz[2 * i + 1, j]
            c0[i + 2, j + 2] = times(*coarse_inverse(i + 2, j + 2), rhs * (1.0 / 64.0))
        return carry

    def send_plane(i):
        copies = []
        for dx in (-1, 1, 0):
            if (dx < 0 and i >= 2) or (dx > 0 and i < cx - 2):
                continue
            to = i + 2 - dx * cx
            for dy in (-1, 1, 0):
                if dx == 0 and dy == 0:
                    continue
                fy, ty, ly = windows(dy, cy, 2, 2)
                d = DIRS.index((dx, dy))
                copy = pltpu.make_async_remote_copy(
                    src_ref=c0.at[i + 2, pl.ds(fy, ly)],
                    dst_ref=c0.at[to, pl.ds(ty, ly)],
                    send_sem=plane_sends.at[i, d],
                    recv_sem=plane_recvs.at[i, d],
                    device_id=(px + dx, py + dy),
                    device_id_type=pl.DeviceIdType.MESH,
                )
                pl.when(there(dx, dy))(copy.start)
                copies.append(((dx, dy), copy))
        return copies

    lax.fori_loop(0, cx + 2, fill_coarse_table, 0)
    sent_planes = []
    for i in range(cx):
        upto = 2 * i + 7
        lax.fori_loop(upto - 2 if i else 0, upto, fill_start, 0)
        lax.fori_loop(upto - 3 if i else 1, upto - 1, sweep, 0)
        lax.fori_loop(upto - 4 if i else LOW, upto - 2, restrict, 0)
        first_correction(i, 0)
        sent_planes += send_plane(i)

    def iterate_out(x, carry):
        for y in range(sizey):
            for half in (0, 1):
                iterate_ref[x, y, half] = w[x + LOW, y + LOW, half] + DAMPING * it0[x + LOW, y + LOW, half]
        return carry

    lax.fori_loop(0, sizex, iterate_out, 0)
    for (dx, dy), copy in sent_planes:
        pl.when(there(-dx, -dy))(copy.wait_recv)

    def coarse_sweep(source, put, i_range, j_range):
        def body(i, carry):
            for j, near in coarse_neighbours(source, i, j_range, first, last):
                change = times(*coarse_inverse(i, j), near * (1.0 / 120.0))
                put(i, j, (1.0 - DAMPING) * source[i, j] + c0[i, j] + change)
            return carry

        lax.fori_loop(*i_range, body, 0)

    def into(ref, off):
        def put(i, j, values):
            ref[i - off, j - off] = values

        return put

    coarse_sweep(c0, into(c1, 0), (1, cx + 3), range(1, cy + 3))
    coarse_sweep(c1, into(c2, 0), (2, cx + 2), range(2, cy + 2))
    sent_third = exchange(1, c2, (cx, cy), 2, 1, 1)
    finish(sent_third)
    coarse_sweep(c2, into(corr_ref, 1), (1, cx + 2), range(1, cy + 2))
    for sent in (sent_labels, sent_third):
        finish_sends(sent)
    for (dx, dy), copy in sent_planes:
        pl.when(there(dx, dy))(copy.wait_send)


def prolong_kernel(iterate_ref, corr_ref, out_hbm, out_ref, flat, store_sems):
    sizex, sizey = iterate_ref.shape[:2]
    stores = []
    nzc = iterate_ref.shape[-1]
    sizez = 2 * nzc
    lane = lax.broadcasted_iota(jnp.int32, (8, nzc), 1)
    first = lane == 0
    row = lax.broadcasted_iota(jnp.int32, (sizez, sizez), 0)
    col = lax.broadcasted_iota(jnp.int32, (sizez, sizez), 1)
    merge = jnp.where(col == jnp.where(row < nzc, 2 * row, 2 * (row - nzc) + 1), 1.0, 0.0).astype(jnp.bfloat16)

    for x in range(sizex):
        i = x // 2 + 1
        across = {}
        for j in range(sizey // 2 + 1):
            across[j] = corr_ref[i, j] if x % 2 else (corr_ref[i - 1, j] + corr_ref[i, j]) * 0.5
        rows = []
        for y in range(sizey):
            j = y // 2 + 1
            odd = across[j] if y % 2 else (across[j - 1] + across[j]) * 0.5
            even = (odd + shift_up(odd, first)) * 0.5
            rows.append(
                jnp.concatenate([iterate_ref[x, y, 0] + even, iterate_ref[x, y, 1] + odd], axis=1)
            )
        block = jnp.concatenate(rows, axis=0)
        top = block.astype(jnp.bfloat16)
        rest = block - top.astype(f32)
        mid = rest.astype(jnp.bfloat16)
        tail = (rest - mid.astype(f32)).astype(jnp.bfloat16)
        merged = (
            jnp.dot(tail, merge, preferred_element_type=f32)
            + jnp.dot(mid, merge, preferred_element_type=f32)
            + jnp.dot(top, merge, preferred_element_type=f32)
        )
        for half in (0, 1):
            flat[x, half] = merged[:, half * nzc : (half + 1) * nzc]
        for f in range(8):
            for half in (0, 1):
                out_ref[x, f // 4, f % 4, :, half * nzc : (half + 1) * nzc] = flat[
                    x, half, pl.ds(f, sizey, stride=8), :
                ]
        stores.append(pltpu.make_async_copy(out_ref.at[x], out_hbm.at[:, :, x], store_sems.at[x]))
        stores[-1].start()
    for store in stores:
        store.wait()


def local(nx, ny, labels, eps_r, eps_i, angles, pick):
    sizex, sizey, sizez = labels.shape
    nzc = sizez // 2
    cx, cy = sizex // 2, sizey // 2
    extx, exty = sizex + LOW + HIGH, sizey + LOW + HIGH
    vmem = pl.BlockSpec(memory_space=pltpu.VMEM)
    hbm = pl.BlockSpec(memory_space=pltpu.HBM)
    iterate, corr = pl.pallas_call(
        functools.partial(cycle_kernel, nx, ny),
        out_shape=(
            jax.ShapeDtypeStruct((sizex, sizey, 2, 8, nzc), f32),
            jax.ShapeDtypeStruct((cx + 1, cy + 1, 8, nzc), f32),
        ),
        in_specs=[hbm] * 5,
        out_specs=(vmem, vmem),
        scratch_shapes=[
            pltpu.VMEM(labels.shape, jnp.int32),
            pltpu.SMEM(eps_r.shape, f32),
            pltpu.SMEM(eps_i.shape, f32),
            pltpu.SMEM(angles.shape, f32),
            pltpu.SMEM(pick.shape, jnp.int32),
            pltpu.SemaphoreType.DMA((5,)),
            pltpu.VMEM((extx, 2 * exty, nzc), f32),
            pltpu.VMEM((6, extx, 2 * exty, nzc), f32),
            pltpu.VMEM((2, cx + 2, 2 * exty, nzc), f32),
            pltpu.VMEM((extx + exty, 2, 8, nzc), f32),
            pltpu.VMEM((extx, exty, 2, 8, nzc), f32),
            pltpu.VMEM((extx, exty, 2, 8, nzc), f32),
            pltpu.VMEM((extx, exty, 2, 8, nzc), f32),
            pltpu.VMEM((sizex + 1, cy, 8, nzc), f32),
            pltpu.VMEM((cx + 4, cy + 4, 8, nzc), f32),
            pltpu.VMEM((cx + 4, cy + 4, 8, nzc), f32),
            pltpu.VMEM((cx + 4, cy + 4, 8, nzc), f32),
            pltpu.SemaphoreType.DMA((2, len(DIRS))),
            pltpu.SemaphoreType.DMA((2, len(DIRS))),
            pltpu.SemaphoreType.DMA((cx, len(DIRS))),
            pltpu.SemaphoreType.DMA((cx, len(DIRS))),
        ],
        compiler_params=pltpu.CompilerParams(
            collective_id=0, has_side_effects=True, vmem_limit_bytes=24 * 2**20
        ),
    )(*(pltpu.with_memory_space_constraint(v, pltpu.HBM) for v in (labels, eps_r, eps_i, angles, pick)))
    return pl.pallas_call(
        prolong_kernel,
        out_shape=jax.ShapeDtypeStruct((2, 4, sizex, sizey, sizez), f32),
        in_specs=[vmem, vmem],
        out_specs=hbm,
        scratch_shapes=[
            pltpu.VMEM((sizex, 2, 4, sizey, sizez), f32),
            pltpu.VMEM((sizex, 2, 8 * sizey, nzc), f32),
            pltpu.SemaphoreType.DMA((sizex,)),
        ],
        compiler_params=pltpu.CompilerParams(vmem_limit_bytes=24 * 2**20),
    )(iterate, corr)


def solution(mesh):
    return jax.shard_map(
        functools.partial(local, mesh.shape["gx"], mesh.shape["gy"]),
        mesh=mesh,
        in_specs=(P("gx", "gy", None), P(), P(), P(), P()),
        out_specs=P(None, None, "gx", "gy", None),
        check_vma=False,
    )
```

```python
import functools

import jax
import jax.numpy as jnp
from jax import lax
from jax.experimental import pallas as pl
from jax.experimental.pallas import tpu as pltpu
from jax.sharding import PartitionSpec as P

MAT = 8
DAMPING = 0.8
WAVE_SQUARED = 0.1
SHIFT_IMAG = 0.5
SOURCE_GAIN = 4.0
CENTRE = 128.0 / 30.0
COARSE_CENTRE = 128.0 / 120.0
LOW, HIGH = 2, 3
DIRS = [(-1, 0), (1, 0), (-1, -1), (1, 1), (-1, 1), (1, -1), (0, -1), (0, 1)]
f32 = jnp.float32


def windows(step, size, low, high):
    if step == 0:
        return low, low, size
    if step > 0:
        return size, 0, low
    return low, low + size, high


def shift_up(values, first):
    return jnp.where(first, 0.0, pltpu.roll(values, 1, 1))


def shift_down(values, last):
    return jnp.where(last, 0.0, pltpu.roll(values, values.shape[1] - 1, 1))


def plane_sums(centre, ends, y):
    side = ends[y] + (centre[y - 1] + centre[y + 1])
    diag = ends[y - 1] + ends[y + 1]
    return 14.0 * side + 3.0 * diag, 14.0 * centre[y] + (3.0 * side + diag)


def fine_neighbours(buf, x, rows, first, last):
    span = range(rows[0] - 1, rows[-1] + 2)
    halves = []
    for half in (0, 1):
        centre = {y: buf[x, y, half] for y in span}
        ends = {y: buf[x - 1, y, half] + buf[x + 1, y, half] for y in span}
        halves.append([plane_sums(centre, ends, y) for y in rows])
    for i, y in enumerate(rows):
        (in_even, out_even), (in_odd, out_odd) = halves[0][i], halves[1][i]
        yield (
            y,
            in_even + (out_odd + shift_up(out_odd, first)),
            in_odd + (out_even + shift_down(out_even, last)),
        )


def coarse_neighbours(buf, x, rows, first, last):
    span = range(rows[0] - 1, rows[-1] + 2)
    centre = {y: buf[x, y] for y in span}
    ends = {y: buf[x - 1, y] + buf[x + 1, y] for y in span}
    for y in rows:
        inner, outer = plane_sums(centre, ends, y)
        yield y, inner + (shift_up(outer, first) + shift_down(outer, last))


def cycle_kernel(
    nx, ny,
    labels_hbm, eps_r_hbm, eps_i_hbm, angles_hbm, pick_hbm,
    iterate_ref, corr_ref,
    labels_ref, eps_r_ref, eps_i_ref, angles_ref, pick_ref, load_sems,
    lab, tab, ctab, ewave, wave, it0, w, yz, c0, c1, c2,
    send_sems, recv_sems, plane_sends, plane_recvs, own, otab,
):
    loads = []
    for k, (source, target) in enumerate((
        (labels_hbm, labels_ref),
        (pick_hbm, pick_ref),
        (angles_hbm, angles_ref),
        (eps_r_hbm, eps_r_ref),
        (eps_i_hbm, eps_i_ref),
    )):
        loads.append(pltpu.make_async_copy(source, target, load_sems.at[k]))
        loads[-1].start()
    sizex, sizey, sizez = labels_ref.shape
    nzc = sizez // 2
    cx, cy = sizex // 2, sizey // 2
    extx, exty = sizex + LOW + HIGH, sizey + LOW + HIGH
    px, py = lax.axis_index("gx"), lax.axis_index("gy")

    def there(dx, dy):
        ok = None
        for step, pos, count in ((dx, px, nx), (dy, py, ny)):
            if step:
                one = (pos > 0) if step < 0 else (pos < count - 1)
                ok = one if ok is None else jnp.logical_and(ok, one)
        return ok

    lab[...] = jnp.full(lab.shape, float(MAT), f32)
    c0[...] = jnp.zeros(c0.shape, f32)
    c2[...] = jnp.zeros(c2.shape, f32)
    barrier = pltpu.get_barrier_semaphore()
    for dx, dy in DIRS:
        @pl.when(there(dx, dy))
        def _():
            pl.semaphore_signal(
                barrier, inc=1, device_id=(px + dx, py + dy), device_id_type=pl.DeviceIdType.MESH
            )

    row = lax.broadcasted_iota(jnp.int32, (sizez, sizez), 0)
    col = lax.broadcasted_iota(jnp.int32, (sizez, sizez), 1)
    split = jnp.where(row == jnp.where(col < nzc, 2 * col, 2 * (col - nzc) + 1), 1.0, 0.0).astype(jnp.bfloat16)
    loads[0].wait()
    mine = labels_ref[...].astype(f32).reshape(sizex * sizey, sizez).astype(jnp.bfloat16)
    mine = jnp.dot(mine, split, preferred_element_type=f32)
    for x in range(sizex):
        for half in (0, 1):
            piece = mine[x * sizey : (x + 1) * sizey, half * nzc : (half + 1) * nzc]
            lab[x + LOW, pl.ds(2 * LOW + half, sizey, stride=2), :] = piece
            own[x, pl.ds(half, sizey, stride=2), :] = piece

    def exchange(phase, buf, sizes, low, high, fold):
        copies = []
        for d, (dx, dy) in enumerate(DIRS):
            fx, tx, lx = windows(dx, sizes[0], low, high)
            fy, ty, ly = windows(dy, sizes[1], low, high)
            out = pltpu.make_async_remote_copy(
                src_ref=buf.at[pl.ds(fx, lx), pl.ds(fold * fy, fold * ly)],
                dst_ref=buf.at[pl.ds(tx, lx), pl.ds(fold * ty, fold * ly)],
                send_sem=send_sems.at[phase, d],
                recv_sem=recv_sems.at[phase, d],
                device_id=(px + dx, py + dy),
                device_id_type=pl.DeviceIdType.MESH,
            )
            copies.append(out)
            pl.when(there(dx, dy))(out.start)
        return copies

    def finish(copies):
        for (dx, dy), copy in zip(DIRS, copies):
            pl.when(there(-dx, -dy))(copy.wait_recv)

    def finish_sends(copies):
        for (dx, dy), copy in zip(DIRS, copies):
            pl.when(there(dx, dy))(copy.wait_send)

    one = jnp.int32(1)
    besides_x = jnp.where(px > 0, one, 0) + jnp.where(px < nx - 1, one, 0)
    besides_y = jnp.where(py > 0, one, 0) + jnp.where(py < ny - 1, one, 0)
    pl.semaphore_wait(barrier, (besides_x + 1) * (besides_y + 1) - 1)
    sent_labels = exchange(0, lab, (sizex, sizey), LOW, HIGH, 2)

    lane = lax.broadcasted_iota(jnp.int32, (8, nzc), 1)
    field = lax.broadcasted_iota(jnp.int32, (8, nzc), 0)
    first, last = lane == 0, lane == nzc - 1
    imag = field >= 4
    sign = jnp.where(imag, 1.0, -1.0)
    column = field % 4
    incidence = jnp.zeros((8, nzc), f32)
    for load in loads[1:]:
        load.wait()
    for c in range(4):
        incidence = jnp.where(column == c, angles_ref[pick_ref[c]], incidence)
    wavenumber = jnp.sqrt(jnp.full((8, nzc), WAVE_SQUARED, f32))
    on_x = lane < nzc // 2
    place = jnp.where(on_x, px * sizex - LOW + lane, py * sizey - LOW + lane - nzc // 2).astype(f32)
    arg = wavenumber * jnp.where(on_x, jnp.cos(incidence), jnp.sin(incidence)) * place
    cos_all, sin_all = jnp.cos(arg), jnp.sin(arg)
    one_all = jnp.where(imag, sin_all, cos_all)
    two_all = jnp.where(imag, cos_all, -sin_all)
    spread = lambda values, at: jnp.broadcast_to(values[:, at : at + 1], (8, nzc))
    for x in range(extx):
        ewave[x, 0] = spread(one_all, x)
        ewave[x, 1] = spread(two_all, x)
    along_y = [
        (spread(cos_all, nzc // 2 + y), spread(sin_all, nzc // 2 + y)) for y in range(exty)
    ]
    for y in range(exty):
        ewave[extx + y, 0], ewave[extx + y, 1] = along_y[y]

    def fill_wave(x, carry):
        wave_one, wave_two = ewave[x, 0], ewave[x, 1]
        for y in range(exty):
            cos_y, sin_y = ewave[extx + y, 0], ewave[extx + y, 1]
            wave[x, y, 0] = cos_y * wave_one + sin_y * wave_two
            wave[x, y, 1] = cos_y * wave_two - sin_y * wave_one
        return carry

    lax.fori_loop(0, extx, fill_wave, 0)
    eps_table = [(eps_r_ref[m], eps_i_ref[m]) for m in range(MAT)]

    def media(label):
        eps_r = jnp.zeros(label.shape, f32)
        eps_i = jnp.zeros(label.shape, f32)
        for m in range(MAT):
            chosen = label == float(m)
            eps_r = jnp.where(chosen, eps_table[m][0], eps_r)
            eps_i = jnp.where(chosen, eps_table[m][1], eps_i)
        med_r = WAVE_SQUARED * (eps_r + SHIFT_IMAG * eps_i)
        med_i = WAVE_SQUARED * (eps_i - SHIFT_IMAG * eps_r)
        return label < MAT - 0.5, eps_r, eps_i, med_r, med_i

    def damped_inverse(inside, med_r, med_i, centre):
        diag = centre - med_r
        scale = jnp.where(inside, DAMPING / (diag * diag + med_i * med_i), 0.0)
        return diag * scale, med_i * scale

    def bcast(ref, at):
        return jnp.broadcast_to(ref[at], (8, nzc))

    def start_body(labels_at, table, rows, off):
        def body(x, carry):
            at_x = x - off
            inside, eps_r, eps_i, med_r, med_i = media(labels_at[at_x])
            inv_r, inv_i = damped_inverse(inside, med_r, med_i, CENTRE)
            src_r = jnp.where(inside, SOURCE_GAIN * (eps_r - 1.0), 0.0)
            src_i = SOURCE_GAIN * eps_i
            table[0, at_x] = inv_r * src_r - inv_i * src_i
            table[1, at_x] = inv_r * src_i + inv_i * src_r
            table[2, at_x] = inv_r * (1.0 / 30.0)
            table[3, at_x] = inv_i * (1.0 / 30.0)
            if off == 0:
                table[4, at_x] = (0.2 * (1.0 - DAMPING)) * src_r
                table[5, at_x] = (0.2 * (1.0 - DAMPING)) * src_i
            for y in rows:
                wave_one, wave_two = wave[x, y, 0], wave[x, y, 1]
                for half in (0, 1):
                    at = (at_x, pl.ds(2 * (y - off) + half, 1))
                    it0[x, y, half] = (
                        bcast(table, (0, *at)) * wave_one + bcast(table, (1, *at)) * wave_two
                    )
            return carry

        return body

    def run(low, high, own_low, own_high, rim_body, own_body):
        for a, b, body in (
            (low, min(high, own_low), rim_body),
            (max(low, own_low), min(high, own_high), own_body),
            (max(low, own_high), high, rim_body),
        ):
            if a < b:
                lax.fori_loop(a, b, body, 0)

    def fill_coarse_table(i, carry):
        inside, _, _, med_r, med_i = media(lab[2 * i + LOW - 1])
        ctab[0, i], ctab[1, i] = damped_inverse(inside, med_r, med_i, COARSE_CENTRE)
        return carry

    def times(real, imaginary, values):
        return real * values + imaginary * (sign * pltpu.roll(values, 4, 0))

    def sweep_body(groups, table, off):
        def body(x, carry):
            for rows in groups:
                for y, even, odd in fine_neighbours(it0, x, rows, first, last):
                    for half, near in enumerate((even, odd)):
                        at = (x - off, pl.ds(2 * (y - off) + half, 1))
                        change = times(bcast(table, (2, *at)), bcast(table, (3, *at)), near)
                        w[x, y, half] = (1.0 + 0.2 - DAMPING) * it0[x, y, half] + change
            return carry

        return body

    endx, endy = LOW + sizex, LOW + sizey
    lax.fori_loop(LOW, endx, start_body(own, otab, range(LOW, endy), LOW), 0)
    lax.fori_loop(LOW + 1, endx - 1, sweep_body([range(LOW + 1, endy - 1)], otab, LOW), 0)
    finish(sent_labels)
    start_rim = start_body(lab, tab, range(exty), 0)
    start_own = start_body(lab, tab, [*range(LOW), *range(endy, exty)], 0)
    sweep_rim = sweep_body([range(1, exty - 1)], tab, 0)
    sweep_own = sweep_body([range(1, LOW + 1), range(endy - 1, exty - 1)], tab, 0)

    def restrict(x, carry):
        in_x = jnp.where(jnp.logical_and(x == LOW + sizex, px == nx - 1), 0.0, 1.0 / 30.0)
        in_xy = jnp.where(py == ny - 1, 0.0, in_x)
        rows = []
        for y, even, odd in fine_neighbours(w, x, range(LOW, LOW + sizey + 1), first, last):
            wave_one, wave_two = wave[x, y, 0], wave[x, y, 1]
            scale = in_xy if y == LOW + sizey else in_x
            both = []
            for half, near in enumerate((even, odd)):
                at = (x, pl.ds(2 * y + half, 1))
                both.append(
                    bcast(tab, (4, *at)) * wave_one + bcast(tab, (5, *at)) * wave_two + scale * near
                )
            rows.append(both)
        for j in range(cy):
            even, odd = (
                (rows[2 * j][half] + rows[2 * j + 2][half]) + 2.0 * rows[2 * j + 1][half]
                for half in (0, 1)
            )
            yz[x - LOW, j] = (even + shift_down(even, last)) + 2.0 * odd
        return carry

    def coarse_inverse(i, j):
        at = (i - 1, pl.ds(2 * (2 * (j - 2) + 1 + LOW) + 1, 1))
        return bcast(ctab, (0, *at)), bcast(ctab, (1, *at))

    def first_correction(i, carry):
        for j in range(cy):
            rhs = (yz[2 * i, j] + yz[2 * i + 2, j]) + 2.0 * yz[2 * i + 1, j]
            c0[i + 2, j + 2] = times(*coarse_inverse(i + 2, j + 2), rhs * (1.0 / 64.0))
        return carry

    def send_plane(i):
        copies = []
        for dx in (-1, 1, 0):
            if (dx < 0 and i >= 2) or (dx > 0 and i < cx - 2):
                continue
            to = i + 2 - dx * cx
            for dy in (-1, 1, 0):
                if dx == 0 and dy == 0:
                    continue
                fy, ty, ly = windows(dy, cy, 2, 2)
                d = DIRS.index((dx, dy))
                copy = pltpu.make_async_remote_copy(
                    src_ref=c0.at[i + 2, pl.ds(fy, ly)],
                    dst_ref=c0.at[to, pl.ds(ty, ly)],
                    send_sem=plane_sends.at[i, d],
                    recv_sem=plane_recvs.at[i, d],
                    device_id=(px + dx, py + dy),
                    device_id_type=pl.DeviceIdType.MESH,
                )
                pl.when(there(dx, dy))(copy.start)
                copies.append(((dx, dy), copy))
        return copies

    sent_planes = []
    for i in range(cx):
        upto = 2 * i + 7
        fill_coarse_table(i + 1, 0)
        run(upto - 2 if i else 0, upto, LOW, endx, start_rim, start_own)
        run(upto - 3 if i else 1, upto - 1, LOW + 1, endx - 1, sweep_rim, sweep_own)
        lax.fori_loop(upto - 4 if i else LOW, upto - 2, restrict, 0)
        first_correction(i, 0)
        sent_planes += send_plane(i)
    fill_coarse_table(0, 0)
    fill_coarse_table(cx + 1, 0)

    def iterate_out(x, carry):
        for y in range(sizey):
            for half in (0, 1):
                iterate_ref[x, y, half] = w[x + LOW, y + LOW, half] + DAMPING * it0[x + LOW, y + LOW, half]
        return carry

    lax.fori_loop(0, sizex, iterate_out, 0)
    for (dx, dy), copy in sent_planes:
        pl.when(there(-dx, -dy))(copy.wait_recv)

    def coarse_sweep(source, put, i_range, j_range):
        def body(i, carry):
            for j, near in coarse_neighbours(source, i, j_range, first, last):
                change = times(*coarse_inverse(i, j), near * (1.0 / 120.0))
                put(i, j, (1.0 - DAMPING) * source[i, j] + c0[i, j] + change)
            return carry

        lax.fori_loop(*i_range, body, 0)

    def into(ref, off):
        def put(i, j, values):
            ref[i - off, j - off] = values

        return put

    coarse_sweep(c0, into(c1, 0), (1, cx + 3), range(1, cy + 3))
    coarse_sweep(c1, into(c2, 0), (2, cx + 2), range(2, cy + 2))
    sent_third = exchange(1, c2, (cx, cy), 2, 1, 1)
    finish(sent_third)
    coarse_sweep(c2, into(corr_ref, 1), (1, cx + 2), range(1, cy + 2))
    for sent in (sent_labels, sent_third):
        finish_sends(sent)
    for (dx, dy), copy in sent_planes:
        pl.when(there(dx, dy))(copy.wait_send)


def prolong_kernel(iterate_ref, corr_ref, out_hbm, out_ref, flat, store_sems):
    sizex, sizey = iterate_ref.shape[:2]
    stores = []
    nzc = iterate_ref.shape[-1]
    sizez = 2 * nzc
    lane = lax.broadcasted_iota(jnp.int32, (8, nzc), 1)
    first = lane == 0
    row = lax.broadcasted_iota(jnp.int32, (sizez, sizez), 0)
    col = lax.broadcasted_iota(jnp.int32, (sizez, sizez), 1)
    merge = jnp.where(col == jnp.where(row < nzc, 2 * row, 2 * (row - nzc) + 1), 1.0, 0.0).astype(jnp.bfloat16)

    for x in range(sizex):
        i = x // 2 + 1
        across = {}
        for j in range(sizey // 2 + 1):
            across[j] = corr_ref[i, j] if x % 2 else (corr_ref[i - 1, j] + corr_ref[i, j]) * 0.5
        rows = []
        for y in range(sizey):
            j = y // 2 + 1
            odd = across[j] if y % 2 else (across[j - 1] + across[j]) * 0.5
            even = (odd + shift_up(odd, first)) * 0.5
            rows.append(
                jnp.concatenate([iterate_ref[x, y, 0] + even, iterate_ref[x, y, 1] + odd], axis=1)
            )
        block = jnp.concatenate(rows, axis=0)
        top = block.astype(jnp.bfloat16)
        rest = block - top.astype(f32)
        mid = rest.astype(jnp.bfloat16)
        tail = (rest - mid.astype(f32)).astype(jnp.bfloat16)
        merged = (
            jnp.dot(tail, merge, preferred_element_type=f32)
            + jnp.dot(mid, merge, preferred_element_type=f32)
            + jnp.dot(top, merge, preferred_element_type=f32)
        )
        for half in (0, 1):
            flat[x, half] = merged[:, half * nzc : (half + 1) * nzc]
        for f in range(8):
            for half in (0, 1):
                out_ref[x, f // 4, f % 4, :, half * nzc : (half + 1) * nzc] = flat[
                    x, half, pl.ds(f, sizey, stride=8), :
                ]
        stores.append(pltpu.make_async_copy(out_ref.at[x], out_hbm.at[:, :, x], store_sems.at[x]))
        stores[-1].start()
    for store in stores:
        store.wait()


def local(nx, ny, labels, eps_r, eps_i, angles, pick):
    sizex, sizey, sizez = labels.shape
    nzc = sizez // 2
    cx, cy = sizex // 2, sizey // 2
    extx, exty = sizex + LOW + HIGH, sizey + LOW + HIGH
    vmem = pl.BlockSpec(memory_space=pltpu.VMEM)
    hbm = pl.BlockSpec(memory_space=pltpu.HBM)
    iterate, corr = pl.pallas_call(
        functools.partial(cycle_kernel, nx, ny),
        out_shape=(
            jax.ShapeDtypeStruct((sizex, sizey, 2, 8, nzc), f32),
            jax.ShapeDtypeStruct((cx + 1, cy + 1, 8, nzc), f32),
        ),
        in_specs=[hbm] * 5,
        out_specs=(vmem, vmem),
        scratch_shapes=[
            pltpu.VMEM(labels.shape, jnp.int32),
            pltpu.SMEM(eps_r.shape, f32),
            pltpu.SMEM(eps_i.shape, f32),
            pltpu.SMEM(angles.shape, f32),
            pltpu.SMEM(pick.shape, jnp.int32),
            pltpu.SemaphoreType.DMA((5,)),
            pltpu.VMEM((extx, 2 * exty, nzc), f32),
            pltpu.VMEM((6, extx, 2 * exty, nzc), f32),
            pltpu.VMEM((2, cx + 2, 2 * exty, nzc), f32),
            pltpu.VMEM((extx + exty, 2, 8, nzc), f32),
            pltpu.VMEM((extx, exty, 2, 8, nzc), f32),
            pltpu.VMEM((extx, exty, 2, 8, nzc), f32),
            pltpu.VMEM((extx, exty, 2, 8, nzc), f32),
            pltpu.VMEM((sizex + 1, cy, 8, nzc), f32),
            pltpu.VMEM((cx + 4, cy + 4, 8, nzc), f32),
            pltpu.VMEM((cx + 4, cy + 4, 8, nzc), f32),
            pltpu.VMEM((cx + 4, cy + 4, 8, nzc), f32),
            pltpu.SemaphoreType.DMA((2, len(DIRS))),
            pltpu.SemaphoreType.DMA((2, len(DIRS))),
            pltpu.SemaphoreType.DMA((cx, len(DIRS))),
            pltpu.SemaphoreType.DMA((cx, len(DIRS))),
            pltpu.VMEM((sizex, 2 * sizey, nzc), f32),
            pltpu.VMEM((4, sizex, 2 * sizey, nzc), f32),
        ],
        compiler_params=pltpu.CompilerParams(
            collective_id=0, has_side_effects=True, vmem_limit_bytes=24 * 2**20
        ),
    )(*(pltpu.with_memory_space_constraint(v, pltpu.HBM) for v in (labels, eps_r, eps_i, angles, pick)))
    return pl.pallas_call(
        prolong_kernel,
        out_shape=jax.ShapeDtypeStruct((2, 4, sizex, sizey, sizez), f32),
        in_specs=[vmem, vmem],
        out_specs=hbm,
        scratch_shapes=[
            pltpu.VMEM((sizex, 2, 4, sizey, sizez), f32),
            pltpu.VMEM((sizex, 2, 8 * sizey, nzc), f32),
            pltpu.SemaphoreType.DMA((sizex,)),
        ],
        compiler_params=pltpu.CompilerParams(vmem_limit_bytes=24 * 2**20),
    )(iterate, corr)


def solution(mesh):
    return jax.shard_map(
        functools.partial(local, mesh.shape["gx"], mesh.shape["gy"]),
        mesh=mesh,
        in_specs=(P("gx", "gy", None), P(), P(), P(), P()),
        out_specs=P(None, None, "gx", "gy", None),
        check_vma=False,
    )
```
